256 devices in a mesh: fn: 64 (over z, x, core), sub: 4 (over y).
Axes of the slice: x: 4, y: 4, z: 8, core: 2. Of those that a mesh axis runs over, the one named last changes fastest.
Arguments:
- coeffs: float32 [8192, 4, 16, 128], P('fn', None, 'sub'), may hold values from -6 to 6
- offsets: int32 [8192], replicated, may hold values from 0 to 1023, as said below
- potential: float32 [1024, 16, 128], P(None, 'sub'), may hold values from -1.5 to 1.5
Outputs:
- gradient: float32 [8192, 4, 16, 128], P('fn', None, 'sub')
The draws below stay inside these ranges and needn't reach their ends.
Inputs may be any that keep to these rules, and one draw needn't show every extreme that they name: `offsets`: Nondecreasing; each grid plane is the first plane of 1 to 15 boxes, both ends reached, on average 8; at most 46 boxes cover any plane (boxes wrap around the periodic wire), and some plane is covered by exactly 46.
All inputs are finite; a program needn't handle non-finite values.
Results may differ from the reference program's by a relative error of at most 0.0003.
Values sent between devices are 32-bit elements; how exact they have to be, the bound alone decides.
No kernel may reach another device: no remote copies, remote signals or barrier semaphores. Data moves between devices by JAX's collectives and lax.ppermute only.
A program may use at most 64 MiB of HBM per device.

```python
import jax
import jax.numpy as jnp
from jax import lax

FN_DEV = 128
PB = 4
CY = 16
CZ = 128
DENS = 8
SWING = 7
NF = 8192
NB = 1024
KMAX = 46
N_FN = 64


def draw_offsets(key, part):
    move_key, spot_key = jax.random.split(key)
    step_sizes = jax.random.randint(move_key, (NB,), -SWING, SWING + 1).astype(jnp.int32)
    center = jax.random.randint(spot_key, (), 6, NB - 1).astype(jnp.int32)
    planted = jnp.array([0, -SWING, -SWING, -SWING, 0, SWING, SWING], jnp.int32)
    plane_ids = jnp.arange(NB, dtype=jnp.int32)
    from_start = plane_ids - (center - 6)
    in_plant = (from_start >= 0) & (from_start < 7)
    plant_values = planted[jnp.clip(from_start, 0, 6)]
    closing = plane_ids == NB - 1

    def advance(earlier, inputs):
        step_size, forced, forced_value, is_closing = inputs
        level = jnp.clip(earlier + step_size, -SWING, SWING).astype(jnp.int32)
        level = jnp.where(forced, forced_value, level)
        level = jnp.where(is_closing, jnp.int32(0), level).astype(jnp.int32)
        return (level, level)
    _, levels = lax.scan(advance, jnp.int32(0), (step_sizes, in_plant, plant_values, closing))
    counts = (DENS + levels - jnp.roll(levels, 1)).astype(jnp.int32)
    endings = jnp.cumsum(counts).astype(jnp.int32)
    func_ids = jnp.arange(NF, dtype=jnp.int32)
    return jnp.searchsorted(endings, func_ids, side='right').astype(jnp.int32)


def block_scale(rng, extent, pieces, least, largest):
    def one(position, shards_of):
        steps = jax.random.uniform(jax.random.fold_in(jax.random.fold_in(rng, 6), position), (shards_of,), jnp.float32, least / len(pieces), largest / len(pieces))
        return jnp.repeat(jnp.exp(steps), extent[position] // shards_of).reshape((-1,) + (1,) * (len(extent) - position - 1))

    loudness = one(*pieces[0])
    for cut in pieces[1:]:
        loudness = loudness * one(*cut)
    return loudness


def noise(stream_key, shape, scale, reach, cuts=(), kind=jnp.bfloat16):
    gain = block_scale(stream_key, shape, cuts, -0.22, 0.18) if cuts else 1.0
    entries = jax.random.normal(stream_key, shape, jnp.float32) * scale * gain
    return jnp.minimum(jnp.maximum(entries, -reach), reach).astype(kind)


def setup_inputs(seed: int = 0) -> dict:
    splits = jax.random.split(jax.random.key(seed), 4)
    coeffs = noise(splits[0], (NF, PB, CY, CZ), 1.0, 6.0, ((0, 64), (2, 4)), jnp.float32)
    offsets = draw_offsets(jax.random.fold_in(splits[3], 71), 0)
    potential = jnp.clip(jax.random.uniform(splits[2], (NB, CY, CZ), jnp.float32, -1.5, 1.5) * block_scale(splits[2], (NB, CY, CZ), ((1, 4),), -0.4, 0.0), -1.5, 1.5)
    return {"coeffs": coeffs, "offsets": offsets, "potential": potential}


penalty = 0.5
highest = lax.Precision.HIGHEST


def kinetic(box_data, padded_y):
    padded_x = jnp.pad(box_data, ((0, 0), (1, 1), (0, 0), (0, 0)))
    padded_z = jnp.pad(box_data, ((0, 0), (0, 0), (0, 0), (1, 1)))
    beside = padded_x[:, 2:] + padded_x[:, :-2]
    beside = beside + padded_y[:, :, 2:] + padded_y[:, :, :-2]
    beside = beside + padded_z[..., 2:] + padded_z[..., :-2]
    return -0.5 * (beside - 6.0 * box_data)


def to_band(gram_block):
    width = gram_block.shape[0]
    row_ids = jnp.arange(width, dtype=jnp.int32)[:, None]
    col_ids = row_ids + jnp.arange(128, dtype=jnp.int32)[None, :] - 64
    inside = (col_ids >= 0) & (col_ids < width)
    picked = jnp.take_along_axis(gram_block, jnp.clip(col_ids, 0, width - 1), axis=1)
    return jnp.where(inside, picked, 0.0)


def from_band(band_rows):
    width = band_rows.shape[0]
    index_map = jnp.arange(width, dtype=jnp.int32)[None, :] - jnp.arange(width, dtype=jnp.int32)[:, None] + 64
    return jnp.take_along_axis(band_rows, index_map, axis=1)


def reference(coeffs, offsets, potential):
    total_funcs = coeffs.shape[0]
    func_ids = jnp.arange(total_funcs, dtype=jnp.int32)
    row_of = (func_ids % N_FN) * FN_DEV + func_ids // N_FN
    box_data = coeffs[row_of]
    padded_y = jnp.pad(box_data, ((0, 0), (0, 0), (1, 1), (0, 0)))
    box_planes = (offsets[:, None] + jnp.arange(PB, dtype=jnp.int32)[None, :]) % NB
    applied = kinetic(box_data, padded_y) + potential[box_planes] * box_data
    bounds = jnp.searchsorted(offsets, jnp.arange(NB + 1, dtype=jnp.int32), side="left").astype(jnp.int32)
    counts = bounds[1:] - bounds[:-1]
    firsts = bounds[:-1]
    plane_all = jnp.arange(NB, dtype=jnp.int32)
    first_rows = firsts[(plane_all - (PB - 1)) % NB]
    live_counts = jnp.zeros((NB,), jnp.int32)
    for back_step in range(PB):
        live_counts = live_counts + counts[(plane_all - back_step) % NB]
    slot_range = jnp.arange(KMAX, dtype=jnp.int32)
    volume = 1.0 / (PB * CY * CZ)

    def plane_data(plane_id):
        is_live = slot_range < live_counts[plane_id]
        members = (first_rows[plane_id] + slot_range) % total_funcs
        piece_index = (plane_id - offsets[members]) % NB
        values = box_data[members, piece_index].reshape(KMAX, CY * CZ) * is_live[:, None]
        images = applied[members, piece_index].reshape(KMAX, CY * CZ) * is_live[:, None]
        return members, piece_index, is_live, values, images

    def plane_band(plane_id):
        members, piece_index, is_live, values, images = plane_data(plane_id)
        gram_block = volume * jnp.dot(values, (images - penalty * values).T, precision=highest)
        return to_band(gram_block), jnp.where(is_live, members, total_funcs)

    blocks, targets = lax.map(plane_band, plane_all)
    band_rows = jnp.zeros((total_funcs, 128), jnp.float32).at[targets.reshape(-1)].add(blocks.reshape(-1, 128), mode="drop")

    def plane_step(plane_id, gradients):
        members, piece_index, is_live, values, images = plane_data(plane_id)
        mixing = from_band(band_rows[members]) * is_live[None, :]
        update = images - jnp.dot(mixing, values, precision=highest) - penalty * values
        target = jnp.where(is_live, members, total_funcs)
        return gradients.at[target, piece_index].set(update.reshape(KMAX, CY, CZ), mode="drop")

    gradients = lax.fori_loop(0, NB, plane_step, jnp.zeros_like(box_data))
    row_ids = jnp.arange(total_funcs, dtype=jnp.int32)
    func_of_row = (row_ids % FN_DEV) * N_FN + row_ids // FN_DEV
    return gradients[func_of_row]
```

```python
import jax
import jax.numpy as jnp
from jax import lax
from jax.experimental import pallas as pl
from jax.experimental.pallas import tpu as pltpu
from jax.sharding import PartitionSpec as P

PB = 4
ROWS = 4
CZ = 128
OWN = 128
HALF = 64
HALO = 48
WIDE = 256
CELLS = ROWS * CZ
BOX = PB * ROWS
PENALTY = 0.5
VOLUME = 1.0 / (PB * 16 * CZ)
VMEM = pltpu.CompilerParams(vmem_limit_bytes=40 * 1024 * 1024)


def split(x):
    hi = x.astype(jnp.bfloat16)
    lo = (x - hi.astype(jnp.float32)).astype(jnp.bfloat16)
    return hi, lo


def own_rows(ref, first, step):
    return jnp.concatenate(
        [ref[pl.ds(par * step + first, HALF, stride=2 * step), :] for par in range(2)], axis=0
    )


def potential_kernel(starts, potential, out):
    planes = potential.shape[0]

    def one(m, carry):
        first = starts[m]
        for p in range(PB):
            plane = first + p
            plane = jnp.where(plane >= planes, plane - planes, plane)
            out[m * PB + p] = potential[plane]
        return carry

    lax.fori_loop(0, OWN, one, 0, unroll=4)


def difference(own_start, wide_start, planes):
    d = wide_start[...] - own_start[...]
    d = jnp.where(d >= planes // 2, d - planes, d)
    return jnp.where(d < -(planes // 2), d + planes, d)


def dot_t(a, b):
    return lax.dot_general(a, b, (((1,), (1,)), ((), ())), preferred_element_type=jnp.float32)


def gram_kernel(
    planes, x, low, high, y_before, y_after, pot, own_start, wide_start,
    band, image, bh, bl, fh, fl, gh, gl, hh, hl,
):
    lane = lax.broadcasted_iota(jnp.int32, (OWN, CZ), 1)
    zero = jnp.zeros((16, CELLS), jnp.bfloat16)
    for q in range(PB):
        for ref in (bh, bl):
            ref[q * WIDE : q * WIDE + 16, :] = zero
            ref[q * WIDE + 240 : q * WIDE + 256, :] = zero
        for y in range(ROWS):
            cols = slice(y * CZ, (y + 1) * CZ)
            for ref, at in ((low, 16), (high, 192)):
                hi, lo = split(ref[pl.ds(q * ROWS + y, HALO, stride=BOX), :])
                bh[q * WIDE + at : q * WIDE + at + HALO, cols] = hi
                bl[q * WIDE + at : q * WIDE + at + HALO, cols] = lo
    for y in range(ROWS):
        cols = slice(y * CZ, (y + 1) * CZ)
        phi = [own_rows(x, p * ROWS + y, BOX) for p in range(PB)]
        acted = []
        for p in range(PB):
            hi, lo = split(phi[p])
            bh[p * WIDE + HALF : p * WIDE + HALF + OWN, cols] = hi
            bl[p * WIDE + HALF : p * WIDE + HALF + OWN, cols] = lo
            up = own_rows(y_before, p, PB) if y == 0 else own_rows(x, p * ROWS + y - 1, BOX)
            down = own_rows(y_after, p, PB) if y == ROWS - 1 else own_rows(x, p * ROWS + y + 1, BOX)
            left = jnp.where(lane == 0, 0.0, pltpu.roll(phi[p], 1, 1))
            right = jnp.where(lane == CZ - 1, 0.0, pltpu.roll(phi[p], CZ - 1, 1))
            acted.append(
                (3.0 - PENALTY + own_rows(pot, p * ROWS + y, BOX)) * phi[p]
                - 0.5 * (up + down + left + right)
            )
        half = [-0.5 * v for v in phi]
        full = [half[0]]
        for p in range(PB):
            v = acted[p]
            if p > 0:
                v = v + half[p - 1]
            if p < PB - 1:
                v = v + half[p + 1]
            image[(p * ROWS + y) * OWN : (p * ROWS + y + 1) * OWN, :] = v
            full.append(v)
        full.append(half[PB - 1])
        for k, v in enumerate(full):
            hi, lo = split(v)
            fh[k * OWN : (k + 1) * OWN, cols] = hi
            fl[k * OWN : (k + 1) * OWN, cols] = lo
        for k in range(3):
            p = k + 1
            v = acted[p] if p == PB - 1 else acted[p] + half[p + 1]
            hi, lo = split(v)
            gh[k * OWN : (k + 1) * OWN, cols] = hi
            gl[k * OWN : (k + 1) * OWN, cols] = lo
            p = k
            v = acted[p] if p == 0 else acted[p] + half[p - 1]
            hi, lo = split(v)
            hh[k * OWN : (k + 1) * OWN, cols] = hi
            hl[k * OWN : (k + 1) * OWN, cols] = lo
    apart = difference(own_start, wide_start, planes)
    total = jnp.zeros((OWN, WIDE), jnp.float32)
    pieces = {
        0: ((fh, fl, 0, 2, -1), (gh, gl, 0, 3, 1)),
        1: ((fh, fl, 0, 6, -1),),
        2: ((fh, fl, 0, 6, -1),),
        3: ((hh, hl, 0, 3, 0), (fh, fl, 4, 2, 3)),
    }
    for q in range(PB):
        right_hi = bh[q * WIDE : (q + 1) * WIDE, :]
        right_lo = bl[q * WIDE : (q + 1) * WIDE, :]
        for hi, lo, at, count, first in pieces[q]:
            rows = slice(at * OWN, (at + count) * OWN)
            r = dot_t(hi[rows, :], right_hi) + dot_t(hi[rows, :], right_lo)
            r = r + dot_t(lo[rows, :], right_hi)
            for k in range(count):
                total = total + jnp.where(
                    apart == first + k - q, r[k * OWN : (k + 1) * OWN, :], 0.0
                )
    total = total * VOLUME
    for b in range(4):
        band[32 * b : 32 * b + 32, :] = total[32 * b : 32 * b + 32, 32 * b + 16 : 32 * b + 144]


def update_kernel(
    planes, b0, b1, b2, b3, image, bh, bl, own_start, wide_start, out, wh, wl, wide
):
    band = b0[...] + b1[...] + b2[...] + b3[...]
    for b in range(4):
        parts = [band[32 * b : 32 * b + 32, :]]
        before, after = 32 * b + 16, 112 - 32 * b
        parts = [jnp.zeros((32, before), jnp.float32), *parts, jnp.zeros((32, after), jnp.float32)]
        wide[32 * b : 32 * b + 32, :] = jnp.concatenate(parts, axis=1)
    mixing = wide[...]
    apart = difference(own_start, wide_start, planes)
    for d in range(1 - PB, PB):
        hi, lo = split(jnp.where(apart == d, mixing, 0.0))
        for p in range(PB):
            q = p - d
            if 0 <= q < PB:
                wh[p * OWN : (p + 1) * OWN, q * WIDE : (q + 1) * WIDE] = hi
                wl[p * OWN : (p + 1) * OWN, q * WIDE : (q + 1) * WIDE] = lo
    def dot(a, b):
        return jnp.dot(a, b, preferred_element_type=jnp.float32)

    r = dot(wh[...], bh[...]) + dot(wh[...], bl[...]) + dot(wl[...], bh[...])
    for p in range(PB):
        for y in range(ROWS):
            v = image[(p * ROWS + y) * OWN : (p * ROWS + y + 1) * OWN, :]
            v = v - r[p * OWN : (p + 1) * OWN, y * CZ : (y + 1) * CZ]
            for par in range(2):
                out[pl.ds(par * BOX + p * ROWS + y, HALF, stride=2 * BOX), :] = v[
                    par * HALF : (par + 1) * HALF
                ]


def shifted(x, axis, step, closed):
    n = lax.axis_size(axis)
    return lax.ppermute(
        x, axis, [(i, (i + step) % n) for i in range(n) if closed or 0 <= i + step < n]
    )


def body(coeffs, offsets, potential):
    peers = lax.axis_size("fn")
    position = lax.axis_index("fn")
    planes = potential.shape[0]
    padded = jnp.concatenate([offsets[-HALF:], offsets, offsets[:HALF]])
    wide_start = lax.dynamic_slice(padded, (position * OWN,), (WIDE,))
    own_start = wide_start[HALF : HALF + OWN]
    by_block = own_start.reshape(2, HALF).T.reshape(OWN)
    wide_start = wide_start[None, :]
    own_start = own_start[:, None]
    f32, bf16 = jnp.float32, jnp.bfloat16
    sds = jax.ShapeDtypeStruct

    pot = pl.pallas_call(
        potential_kernel,
        out_shape=sds((OWN * PB, ROWS, CZ), f32),
        in_specs=[
            pl.BlockSpec(memory_space=pltpu.SMEM),
            pl.BlockSpec(memory_space=pltpu.VMEM),
        ],
        out_specs=pl.BlockSpec(memory_space=pltpu.VMEM),
        compiler_params=VMEM,
        cost_estimate=pl.CostEstimate(flops=0, bytes_accessed=4 << 20, transcendentals=0),
        name="box_potential",
    )(by_block, potential)
    pot = pot.reshape(OWN * BOX, CZ)

    x = lax.all_to_all(
        coeffs.reshape(peers, 2 * BOX, CZ), "fn", split_axis=0, concat_axis=0, tiled=True
    )
    boxes = x.reshape(HALF, 2, BOX, CZ)
    rows = x.reshape(OWN * PB, ROWS, CZ)
    y_before = shifted(rows[:, ROWS - 1], "sub", 1, False)
    y_after = shifted(rows[:, 0], "sub", -1, False)
    low = shifted(boxes[HALF - HALO :, 1].reshape(HALO * BOX, CZ), "fn", 1, True)
    high = shifted(boxes[:HALO, 0].reshape(HALO * BOX, CZ), "fn", -1, True)

    band, image, bh, bl = pl.pallas_call(
        lambda *refs: gram_kernel(planes, *refs),
        out_shape=(
            sds((OWN, CZ), f32),
            sds((BOX * OWN, CZ), f32),
            sds((PB * WIDE, CELLS), bf16),
            sds((PB * WIDE, CELLS), bf16),
        ),
        scratch_shapes=[
            pltpu.VMEM((6 * OWN, CELLS), bf16),
            pltpu.VMEM((6 * OWN, CELLS), bf16),
            pltpu.VMEM((3 * OWN, CELLS), bf16),
            pltpu.VMEM((3 * OWN, CELLS), bf16),
            pltpu.VMEM((3 * OWN, CELLS), bf16),
            pltpu.VMEM((3 * OWN, CELLS), bf16),
        ],
        compiler_params=VMEM,
        cost_estimate=pl.CostEstimate(
            flops=3 << 30, bytes_accessed=8 << 20, transcendentals=0
        ),
        name="band",
    )(x.reshape(OWN * BOX, CZ), low, high, y_before, y_after, pot, own_start, wide_start)

    bands = [band] + [shifted(band, "sub", k, True) for k in (1, 2, 3)]
    gradient = pl.pallas_call(
        lambda *refs: update_kernel(planes, *refs),
        out_shape=sds((OWN * BOX, CZ), f32),
        scratch_shapes=[
            pltpu.VMEM((PB * OWN, PB * WIDE), bf16),
            pltpu.VMEM((PB * OWN, PB * WIDE), bf16),
            pltpu.VMEM((OWN, WIDE), f32),
        ],
        compiler_params=VMEM,
        cost_estimate=pl.CostEstimate(
            flops=2 << 30, bytes_accessed=5 << 20, transcendentals=0
        ),
        name="gradient",
    )(*bands, image, bh, bl, own_start, wide_start)
    back = lax.all_to_all(
        gradient.reshape(peers, 2 * BOX, CZ), "fn", split_axis=0, concat_axis=0, tiled=True
    )
    return back.reshape(coeffs.shape)


def solution(mesh):
    return jax.shard_map(
        body,
        mesh=mesh,
        in_specs=(P("fn", None, "sub", None), P(), P(None, "sub", None)),
        out_specs=P("fn", None, "sub", None),
        check_vma=False,
    )
```

```python
import jax
import jax.numpy as jnp
from jax import lax
from jax.experimental import pallas as pl
from jax.experimental.pallas import tpu as pltpu
from jax.sharding import PartitionSpec as P

PB = 4
ROWS = 4
CZ = 128
OWN = 128
HALF = 64
HALO = 48
WIDE = 256
CELLS = ROWS * CZ
BOX = PB * ROWS
PENALTY = 0.5
INNER = (1, 2)
OUTER = (0, 3)
ORDER = INNER + OUTER
VOLUME = 1.0 / (PB * 16 * CZ)


def vmem(mib):
    return pltpu.CompilerParams(vmem_limit_bytes=mib << 20)


def split(x):
    hi = x.astype(jnp.bfloat16)
    lo = (x - hi.astype(jnp.float32)).astype(jnp.bfloat16)
    return hi, lo


def own_rows(ref, first, step):
    return jnp.concatenate(
        [ref[pl.ds(par * step + first, HALF, stride=2 * step), :] for par in range(2)], axis=0
    )


def potential_kernel(starts, potential, out):
    planes = potential.shape[0]

    for par in range(2):

        def one(f, carry):
            first = starts[par * HALF + f]
            for p in range(PB):
                plane = first + p
                plane = jnp.where(plane >= planes, plane - planes, plane)
                out[(f * 2 + par) * PB + p] = potential[plane]
            return carry

        lax.fori_loop(0, HALF, one, 0, unroll=4)


def edge_kernel(x, first, last, low, high):
    rows, at = PB * OWN, lax.axis_index("sub")
    first[...] = jnp.where(at == 0, 0.0, x[pl.ds(0, rows, stride=ROWS), :])
    last[...] = jnp.where(at == lax.axis_size("sub") - 1, 0.0, x[pl.ds(ROWS - 1, rows, stride=ROWS), :])
    for k in range(HALO):
        to = slice(k * BOX, (k + 1) * BOX)
        low_at = (HALF - HALO + k) * 2 * BOX + BOX
        low[to, :] = x[low_at : low_at + BOX, :]
        high[to, :] = x[k * 2 * BOX : k * 2 * BOX + BOX, :]


def difference(own_start, wide_start, planes):
    d = wide_start[...] - own_start[...]
    d = jnp.where(d >= planes // 2, d - planes, d)
    return jnp.where(d < -(planes // 2), d + planes, d)


def dot_t(a, b):
    return lax.dot_general(a, b, (((1,), (1,)), ((), ())), preferred_element_type=jnp.float32)


def put(hi_ref, lo_ref, k, cols, v):
    hi, lo = split(v)
    hi_ref[k * OWN : (k + 1) * OWN, cols] = hi
    lo_ref[k * OWN : (k + 1) * OWN, cols] = lo


def act(x, pot, p, y, phi):
    lane = lax.broadcasted_iota(jnp.int32, (OWN, CZ), 1)
    first = p * ROWS + y
    beside = jnp.where(lane == 0, 0.0, pltpu.roll(phi, 1, 1))
    beside = beside + jnp.where(lane == CZ - 1, 0.0, pltpu.roll(phi, CZ - 1, 1))
    if y > 0:
        beside = beside + own_rows(x, first - 1, BOX)
    if y < ROWS - 1:
        beside = beside + own_rows(x, first + 1, BOX)
    return (3.0 - PENALTY + own_rows(pot, first, BOX)) * phi - 0.5 * beside


def left_sides(at, phi, acted, image, fh, fl, gh, gl, hh, hl):
    cols = slice(at * CZ, (at + 1) * CZ)
    half = [-0.5 * v for v in phi]
    put(fh, fl, 0, cols, half[0])
    put(fh, fl, 5, cols, half[PB - 1])
    for p in range(PB):
        v = acted[p]
        if p > 0:
            v = v + half[p - 1]
        if p < PB - 1:
            v = v + half[p + 1]
        image[(p * 2 + at) * OWN : (p * 2 + at + 1) * OWN, :] = v
        put(fh, fl, p + 1, cols, v)
    for k in range(3):
        p = k + 1
        put(gh, gl, k, cols, acted[p] if p == PB - 1 else acted[p] + half[p + 1])
        put(hh, hl, k, cols, acted[k] if k == 0 else acted[k] + half[k - 1])


def inner_kernel(x, pot_any, bh, bl, image, partial, fh, fl, gh, gl, hh, hl, pot, sem):
    copy = pltpu.make_async_copy(pot_any, pot, sem)
    copy.start()
    for p in range(PB):
        for at, y in enumerate(ORDER):
            cols = slice(at * CZ, (at + 1) * CZ)
            hi, lo = split(own_rows(x, p * ROWS + y, BOX))
            bh[p, :, cols] = hi
            bl[p, :, cols] = lo
    copy.wait()
    for at, y in enumerate(INNER):
        phi = [own_rows(x, p * ROWS + y, BOX) for p in range(PB)]
        acted = [act(x, pot, p, y, phi[p]) for p in range(PB)]
        left_sides(at, phi, acted, image, fh, fl, gh, gl, hh, hl)
    for at, y in enumerate(OUTER):
        for p in range(PB):
            v = act(x, pot, p, y, own_rows(x, p * ROWS + y, BOX))
            partial[(p * 2 + at) * OWN : (p * 2 + at + 1) * OWN, :] = v


def band_kernel(
    planes, x, low, high, y_before, y_after, partial, own_start, wide_start, own_bh, own_bl,
    fh_in, fl_in, gh_in, gl_in, hh_in, hl_in,
    band, image, bh, bl, fh, fl, gh, gl, hh, hl,
):
    for at, (y, beyond) in enumerate(zip(OUTER, (y_before, y_after))):
        phi = [own_rows(x, p * ROWS + y, BOX) for p in range(PB)]
        acted = [
            partial[(p * 2 + at) * OWN : (p * 2 + at + 1) * OWN, :] - 0.5 * own_rows(beyond, p, PB)
            for p in range(PB)
        ]
        left_sides(at, phi, acted, image, fh, fl, gh, gl, hh, hl)
    zero = jnp.zeros((16, CELLS), jnp.bfloat16)
    for q in range(PB):
        for ref, own in ((bh, own_bh), (bl, own_bl)):
            ref[q, 0:16, :] = zero
            ref[q, HALF : HALF + OWN, :] = own[q]
            ref[q, WIDE - 16 :, :] = zero
        for at, y in enumerate(ORDER):
            cols = slice(at * CZ, (at + 1) * CZ)
            for ref, to in ((low, 16), (high, HALF + OWN)):
                hi, lo = split(ref[pl.ds(q * ROWS + y, HALO, stride=BOX), :])
                bh[q, to : to + HALO, cols] = hi
                bl[q, to : to + HALO, cols] = lo
    apart = difference(own_start, wide_start, planes)
    total = jnp.zeros((OWN, WIDE), jnp.float32)
    full = ((fh_in, fl_in), (fh, fl))
    pieces = {
        0: ((full, 0, 2, -1), (((gh_in, gl_in), (gh, gl)), 0, 3, 1)),
        1: ((full, 0, 6, -1),),
        2: ((full, 0, 6, -1),),
        3: ((((hh_in, hl_in), (hh, hl)), 0, 3, 0), (full, 4, 2, 3)),
    }
    for q in range(PB):
        for sides, at, count, first in pieces[q]:
            rows = slice(at * OWN, (at + count) * OWN)
            r = None
            for side, (hi, lo) in enumerate(sides):
                cols = slice(side * 2 * CZ, (side + 1) * 2 * CZ)
                right_hi, right_lo = bh[q, :, cols], bl[q, :, cols]
                v = dot_t(hi[rows, :], right_hi) + dot_t(hi[rows, :], right_lo)
                v = v + dot_t(lo[rows, :], right_hi)
                r = v if r is None else r + v
            for k in range(count):
                total = total + jnp.where(
                    apart == first + k - q, r[k * OWN : (k + 1) * OWN, :], 0.0
                )
    total = total * VOLUME
    for b in range(4):
        band[32 * b : 32 * b + 32, :] = total[32 * b : 32 * b + 32, 32 * b + 16 : 32 * b + 144]


def update_kernel(
    planes, b0, b1, b2, b3, image_in, image_out, bh, bl, own_start, wide_start, out, wh, wl, wide
):
    band = b0[...] + b1[...] + b2[...] + b3[...]
    for b in range(4):
        parts = [band[32 * b : 32 * b + 32, :]]
        before, after = 32 * b + 16, 112 - 32 * b
        parts = [jnp.zeros((32, before), jnp.float32), *parts, jnp.zeros((32, after), jnp.float32)]
        wide[32 * b : 32 * b + 32, :] = jnp.concatenate(parts, axis=1)
    mixing = wide[...]
    apart = difference(own_start, wide_start, planes)
    for d in range(1 - PB, PB):
        hi, lo = split(jnp.where(apart == d, mixing, 0.0))
        for p in range(PB):
            q = p - d
            if 0 <= q < PB:
                wh[p * OWN : (p + 1) * OWN, q * WIDE : (q + 1) * WIDE] = hi
                wl[p * OWN : (p + 1) * OWN, q * WIDE : (q + 1) * WIDE] = lo
    def dot(a, b):
        return jnp.dot(a, b, preferred_element_type=jnp.float32)

    r = dot(wh[...], bh[...]) + dot(wh[...], bl[...]) + dot(wl[...], bh[...])
    for p in range(PB):
        for at, y in enumerate(ORDER):
            image = (image_in, image_out)[at // 2]
            first = (p * 2 + at % 2) * OWN
            v = image[first : first + OWN, :]
            v = v - r[p * OWN : (p + 1) * OWN, at * CZ : (at + 1) * CZ]
            for par in range(2):
                out[pl.ds(par * BOX + p * ROWS + y, HALF, stride=2 * BOX), :] = v[
                    par * HALF : (par + 1) * HALF
                ]


def shifted(x, axis, step):
    n = lax.axis_size(axis)
    return lax.ppermute(x, axis, [(i, (i + step) % n) for i in range(n)])


def body(coeffs, offsets, potential):
    peers = lax.axis_size("fn")
    position = lax.axis_index("fn")
    planes = potential.shape[0]
    padded = jnp.concatenate([offsets[-HALF:], offsets, offsets[:HALF]])
    wide_start = lax.dynamic_slice(padded, (position * OWN,), (WIDE,))
    own_start = wide_start[HALF : HALF + OWN]
    f32, bf16 = jnp.float32, jnp.bfloat16
    sds = jax.ShapeDtypeStruct

    def cost(flops, size):
        return pl.CostEstimate(flops=flops, bytes_accessed=size, transcendentals=0)

    pot = pl.pallas_call(
        potential_kernel,
        out_shape=sds((OWN * PB, ROWS, CZ), f32),
        in_specs=[
            pl.BlockSpec(memory_space=pltpu.SMEM),
            pl.BlockSpec(memory_space=pltpu.VMEM),
        ],
        compiler_params=vmem(10),
        cost_estimate=cost(0, 4 << 20),
        name="box_potential",
    )(own_start, potential)
    pot = pot.reshape(OWN * BOX, CZ)
    wide_start = wide_start[None, :]
    own_start = own_start[:, None]

    x = lax.all_to_all(
        coeffs.reshape(peers, 2 * BOX, CZ), "fn", split_axis=0, concat_axis=0, tiled=True
    )
    x, pot, own_start, wide_start = lax.optimization_barrier((x, pot, own_start, wide_start))
    x = x.reshape(OWN * BOX, CZ)
    edge, halo = sds((OWN * PB, CZ), f32), sds((HALO * BOX, CZ), f32)
    first, last, low, high = pl.pallas_call(
        edge_kernel,
        out_shape=(edge, edge, halo, halo),
        compiler_params=vmem(10),
        cost_estimate=cost(0, 2 << 20),
        name="edges",
    )(x)
    y_before = shifted(last, "sub", 1)
    y_after = shifted(first, "sub", -1)
    low = shifted(low, "fn", 1)
    high = shifted(high, "fn", -1)

    image = sds((PB * 2 * OWN, CZ), f32)
    left = [sds((n * OWN, 2 * CZ), bf16) for n in (6, 6, 3, 3, 3, 3)]
    own_bh, own_bl, image_in, partial, *ready = pl.pallas_call(
        inner_kernel,
        out_shape=(sds((PB, OWN, CELLS), bf16), sds((PB, OWN, CELLS), bf16), image, image, *left),
        in_specs=[pl.BlockSpec(memory_space=pltpu.VMEM), pl.BlockSpec(memory_space=pl.ANY)],
        scratch_shapes=[pltpu.VMEM((OWN * BOX, CZ), f32), pltpu.SemaphoreType.DMA],
        compiler_params=vmem(20),
        cost_estimate=cost(1 << 30, 5 << 20),
        name="inner_rows",
    )(x, pot)

    band, image_out, bh, bl = pl.pallas_call(
        lambda *refs: band_kernel(planes, *refs),
        out_shape=(
            sds((OWN, CZ), f32),
            image,
            sds((PB, WIDE, CELLS), bf16),
            sds((PB, WIDE, CELLS), bf16),
        ),
        scratch_shapes=[pltpu.VMEM(v.shape, v.dtype) for v in left],
        compiler_params=vmem(20),
        cost_estimate=cost(3 << 30, 8 << 20),
        name="band",
    )(x, low, high, y_before, y_after, partial, own_start, wide_start, own_bh, own_bl, *ready)

    bands = [band] + [shifted(band, "sub", k) for k in (1, 2, 3)]
    gradient = pl.pallas_call(
        lambda *refs: update_kernel(planes, *refs),
        out_shape=sds((OWN * BOX, CZ), f32),
        scratch_shapes=[
            pltpu.VMEM((PB * OWN, PB * WIDE), bf16),
            pltpu.VMEM((PB * OWN, PB * WIDE), bf16),
            pltpu.VMEM((OWN, WIDE), f32),
        ],
        compiler_params=vmem(20),
        cost_estimate=cost(2 << 30, 5 << 20),
        name="gradient",
    )(
        *bands, image_in, image_out, bh.reshape(PB * WIDE, CELLS), bl.reshape(PB * WIDE, CELLS),
        own_start, wide_start,
    )
    back = lax.all_to_all(
        gradient.reshape(peers, 2, PB, ROWS, CZ), "fn", split_axis=0, concat_axis=0, tiled=True
    )
    return back.reshape(coeffs.shape)


def solution(mesh):
    return jax.shard_map(
        body,
        mesh=mesh,
        in_specs=(P("fn", None, "sub", None), P(), P(None, "sub", None)),
        out_specs=P("fn", None, "sub", None),
        check_vma=False,
    )
```

```python
import jax
import jax.numpy as jnp
from jax import lax
from jax.experimental import pallas as pl
from jax.experimental.pallas import tpu as pltpu
from jax.sharding import PartitionSpec as P

PB = 4
ROWS = 4
CZ = 128
OWN = 128
HALF = 64
HALO = 48
WIDE = 256
CELLS = ROWS * CZ
BOX = PB * ROWS
PENALTY = 0.5
INNER = (1, 2)
OUTER = (0, 3)
ORDER = INNER + OUTER
LINE = 8
VOLUME = 1.0 / (PB * 16 * CZ)


def vmem(mib):
    return pltpu.CompilerParams(vmem_limit_bytes=mib << 20)


def split(x):
    hi = x.astype(jnp.bfloat16)
    lo = (x - hi.astype(jnp.float32)).astype(jnp.bfloat16)
    return hi, lo


def own_rows(ref, first, step):
    return jnp.concatenate(
        [ref[pl.ds(par * step + first, HALF, stride=2 * step), :] for par in range(2)], axis=0
    )


def potential_kernel(starts, potential, out):
    planes = potential.shape[0]

    def one(n, carry):
        first = starts[n]
        for p in range(PB):
            plane = first + p
            plane = jnp.where(plane >= planes, plane - planes, plane)
            v = potential[plane]
            for y in range(ROWS):
                out[pl.ds((p * ROWS + y) * OWN + n, 1), :] = v[y : y + 1, :]
        return carry

    lax.fori_loop(0, OWN, one, 0, unroll=4)


def edge_kernel(x, first, last, low, high):
    at = lax.axis_index("sub")
    for p in range(PB):
        to = slice(p * OWN, (p + 1) * OWN)
        first[to, :] = jnp.where(at == 0, 0.0, own_rows(x, p * ROWS, BOX))
        v = own_rows(x, p * ROWS + ROWS - 1, BOX)
        last[to, :] = jnp.where(at == lax.axis_size("sub") - 1, 0.0, v)
    for k in range(HALO):
        to = slice(k * BOX, (k + 1) * BOX)
        low_at = (HALF - HALO + k) * 2 * BOX + BOX
        low[to, :] = x[low_at : low_at + BOX, :]
        high[to, :] = x[k * 2 * BOX : k * 2 * BOX + BOX, :]


def difference(own_start, wide_start, planes):
    d = wide_start[...] - own_start[...]
    d = jnp.where(d >= planes // 2, d - planes, d)
    return jnp.where(d < -(planes // 2), d + planes, d)


def dot_t(a, b):
    return lax.dot_general(a, b, (((1,), (1,)), ((), ())), preferred_element_type=jnp.float32)


def block(ref, p, y):
    at = (p * ROWS + y) * OWN
    return ref[at : at + OWN, :]


def put(hi_ref, lo_ref, k, cols, v):
    hi, lo = split(v)
    hi_ref[k * OWN : (k + 1) * OWN, cols] = hi
    lo_ref[k * OWN : (k + 1) * OWN, cols] = lo


def act(xs, pot, p, y):
    lane = lax.broadcasted_iota(jnp.int32, (OWN, CZ), 1)
    phi = block(xs, p, y)
    beside = jnp.where(lane == 0, 0.0, pltpu.roll(phi, 1, 1))
    beside = beside + jnp.where(lane == CZ - 1, 0.0, pltpu.roll(phi, CZ - 1, 1))
    if y > 0:
        beside = beside + block(xs, p, y - 1)
    if y < ROWS - 1:
        beside = beside + block(xs, p, y + 1)
    return (3.0 - PENALTY + block(pot, p, y)) * phi - 0.5 * beside


def left_sides(at, phi, acted, image, fh, fl, gh, gl, hh, hl):
    cols = slice(at * CZ, (at + 1) * CZ)
    half = [-0.5 * v for v in phi]
    put(fh, fl, 0, cols, half[0])
    put(fh, fl, 5, cols, half[PB - 1])
    for p in range(PB):
        v = acted[p]
        if p > 0:
            v = v + half[p - 1]
        if p < PB - 1:
            v = v + half[p + 1]
        image[(p * 2 + at) * OWN : (p * 2 + at + 1) * OWN, :] = v
        put(fh, fl, p + 1, cols, v)
    for k in range(3):
        p = k + 1
        put(gh, gl, k, cols, acted[p] if p == PB - 1 else acted[p] + half[p + 1])
        put(hh, hl, k, cols, acted[k] if k == 0 else acted[k] + half[k - 1])


def inner_kernel(x, pot_any, bh, bl, xs, image, partial, fh, fl, gh, gl, hh, hl, pot, sem):
    copy = pltpu.make_async_copy(pot_any, pot, sem)
    copy.start()
    for p in range(PB):
        for at, y in enumerate(ORDER):
            cols = slice(at * CZ, (at + 1) * CZ)
            v = own_rows(x, p * ROWS + y, BOX)
            to = (p * ROWS + y) * OWN
            xs[to : to + OWN, :] = v
            hi, lo = split(v)
            bh[p, :, cols] = hi
            bl[p, :, cols] = lo
    copy.wait()
    for at, y in enumerate(INNER):
        phi = [block(xs, p, y) for p in range(PB)]
        acted = [act(xs, pot, p, y) for p in range(PB)]
        left_sides(at, phi, acted, image, fh, fl, gh, gl, hh, hl)
    for at, y in enumerate(OUTER):
        for p in range(PB):
            partial[(p * 2 + at) * OWN : (p * 2 + at + 1) * OWN, :] = act(xs, pot, p, y)


def outer_rows(xs, y_before, y_after, partial, image, fh, fl, gh, gl, hh, hl):
    for at, (y, beyond) in enumerate(zip(OUTER, (y_before, y_after))):
        phi = [block(xs, p, y) for p in range(PB)]
        acted = [
            partial[(p * 2 + at) * OWN : (p * 2 + at + 1) * OWN, :]
            - 0.5 * beyond[p * OWN : (p + 1) * OWN, :]
            for p in range(PB)
        ]
        left_sides(at, phi, acted, image, fh, fl, gh, gl, hh, hl)


def products(total, apart, bh, bl, side, fh, fl, gh, gl, hh, hl):
    cols = slice(side * 2 * CZ, (side + 1) * 2 * CZ)
    pieces = {
        0: ((fh, fl, 0, 2, -1), (gh, gl, 0, 3, 1)),
        1: ((fh, fl, 0, 6, -1),),
        2: ((fh, fl, 0, 6, -1),),
        3: ((hh, hl, 0, 3, 0), (fh, fl, 4, 2, 3)),
    }
    for q in range(PB):
        right_hi, right_lo = bh[q, :, cols], bl[q, :, cols]
        for hi, lo, at, count, first in pieces[q]:
            rows = slice(at * OWN, (at + count) * OWN)
            r = dot_t(hi[rows, :], right_hi) + dot_t(hi[rows, :], right_lo)
            r = r + dot_t(lo[rows, :], right_hi)
            for k in range(count):
                total = total + jnp.where(
                    apart == first + k - q, r[k * OWN : (k + 1) * OWN, :], 0.0
                )
    return total


def inner_band_kernel(
    planes, low, high, own_start, wide_start, own_bh, own_bl, fh, fl, gh, gl, hh, hl,
    bh, bl, total,
):
    zero = jnp.zeros((16, CELLS), jnp.bfloat16)
    for q in range(PB):
        for ref, own in ((bh, own_bh), (bl, own_bl)):
            ref[q, 0:16, :] = zero
            ref[q, HALF : HALF + OWN, :] = own[q]
            ref[q, WIDE - 16 :, :] = zero
        for at, y in enumerate(ORDER):
            cols = slice(at * CZ, (at + 1) * CZ)
            for ref, to in ((low, 16), (high, HALF + OWN)):
                hi, lo = split(ref[pl.ds(q * ROWS + y, HALO, stride=BOX), :])
                bh[q, to : to + HALO, cols] = hi
                bl[q, to : to + HALO, cols] = lo
    apart = difference(own_start, wide_start, planes)
    start = jnp.zeros((OWN, WIDE), jnp.float32)
    total[...] = products(start, apart, bh, bl, 0, fh, fl, gh, gl, hh, hl)


def band_kernel(
    planes, xs, y_before, y_after, partial, own_start, wide_start, bh, bl, earlier,
    band, image, fh, fl, gh, gl, hh, hl,
):
    outer_rows(xs, y_before, y_after, partial, image, fh, fl, gh, gl, hh, hl)
    apart = difference(own_start, wide_start, planes)
    total = products(earlier[...], apart, bh, bl, 1, fh, fl, gh, gl, hh, hl) * VOLUME
    for b in range(4):
        band[32 * b : 32 * b + 32, :] = total[32 * b : 32 * b + 32, 32 * b + 16 : 32 * b + 144]


def update_kernel(
    planes, b0, b1, b2, b3, image_in, image_out, bh, bl, own_start, wide_start, out, wh, wl, wide
):
    band = b0[...] + b1[...] + b2[...] + b3[...]
    for b in range(4):
        parts = [band[32 * b : 32 * b + 32, :]]
        before, after = 32 * b + 16, 112 - 32 * b
        parts = [jnp.zeros((32, before), jnp.float32), *parts, jnp.zeros((32, after), jnp.float32)]
        wide[32 * b : 32 * b + 32, :] = jnp.concatenate(parts, axis=1)
    mixing = wide[...]
    apart = difference(own_start, wide_start, planes)
    for d in range(1 - PB, PB):
        hi, lo = split(jnp.where(apart == d, mixing, 0.0))
        for p in range(PB):
            q = p - d
            if 0 <= q < PB:
                wh[p * OWN : (p + 1) * OWN, q * WIDE : (q + 1) * WIDE] = hi
                wl[p * OWN : (p + 1) * OWN, q * WIDE : (q + 1) * WIDE] = lo
    def dot(a, b):
        return jnp.dot(a, b, preferred_element_type=jnp.float32)

    r = dot(wh[...], bh[...]) + dot(wh[...], bl[...]) + dot(wl[...], bh[...])
    for p in range(PB):
        for at, y in enumerate(ORDER):
            image = (image_in, image_out)[at // 2]
            first = (p * 2 + at % 2) * OWN
            v = image[first : first + OWN, :]
            v = v - r[p * OWN : (p + 1) * OWN, at * CZ : (at + 1) * CZ]
            for par in range(2):
                out[pl.ds(par * BOX + p * ROWS + y, HALF, stride=2 * BOX), :] = v[
                    par * HALF : (par + 1) * HALF
                ]


def snake(k):
    return k if k // LINE % 2 == 0 else k // LINE * LINE + LINE - 1 - k % LINE


def shifted(x, axis, step):
    n = lax.axis_size(axis)
    at = snake if axis == "fn" else int
    return lax.ppermute(x, axis, [(at(i), at((i + step) % n)) for i in range(n)])


def exchanged(x):
    order = [snake(k) for k in range(lax.axis_size("fn"))]
    return lax.all_to_all(
        x, "fn", split_axis=0, concat_axis=0, axis_index_groups=[order], tiled=True
    )


def body(coeffs, offsets, potential):
    peers = lax.axis_size("fn")
    position = lax.axis_index("fn")
    planes = potential.shape[0]
    padded = jnp.concatenate([offsets[-HALF:], offsets, offsets[:HALF]])
    line, along = position // LINE, position % LINE
    number = jnp.where(line % 2 == 0, position, line * LINE + LINE - 1 - along)
    wide_start = lax.dynamic_slice(padded, (number * OWN,), (WIDE,)).reshape(-1, 2, LINE)
    wide_start = jnp.stack([wide_start[:, 0], wide_start[:, 1, ::-1]], axis=1).reshape(WIDE)
    own_start = wide_start[HALF : HALF + OWN]
    f32, bf16 = jnp.float32, jnp.bfloat16
    sds = jax.ShapeDtypeStruct

    def cost(flops, size):
        return pl.CostEstimate(flops=flops, bytes_accessed=size, transcendentals=0)

    pot = pl.pallas_call(
        potential_kernel,
        out_shape=sds((OWN * BOX, CZ), f32),
        in_specs=[
            pl.BlockSpec(memory_space=pltpu.SMEM),
            pl.BlockSpec(memory_space=pltpu.VMEM),
        ],
        compiler_params=vmem(10),
        cost_estimate=cost(0, 4 << 20),
        name="box_potential",
    )(own_start, potential)
    wide_start = wide_start[None, :]
    own_start = own_start[:, None]

    x = exchanged(coeffs.reshape(peers, 2 * BOX, CZ))
    x, pot, own_start, wide_start = lax.optimization_barrier((x, pot, own_start, wide_start))
    x = x.reshape(OWN * BOX, CZ)
    edge, halo = sds((OWN * PB, CZ), f32), sds((HALO * BOX, CZ), f32)
    first, last, low, high = pl.pallas_call(
        edge_kernel,
        out_shape=(edge, edge, halo, halo),
        compiler_params=vmem(10),
        cost_estimate=cost(0, 2 << 20),
        name="edges",
    )(x)
    y_before = shifted(last, "sub", 1)
    y_after = shifted(first, "sub", -1)
    low = shifted(low, "fn", 1)
    high = shifted(high, "fn", -1)

    image = sds((PB * 2 * OWN, CZ), f32)
    left = [sds((n * OWN, 2 * CZ), bf16) for n in (6, 6, 3, 3, 3, 3)]
    own = sds((PB, OWN, CELLS), bf16)
    own_bh, own_bl, xs, image_in, partial, *inner = pl.pallas_call(
        inner_kernel,
        out_shape=(own, own, sds((OWN * BOX, CZ), f32), image, image, *left),
        in_specs=[pl.BlockSpec(memory_space=pltpu.VMEM), pl.BlockSpec(memory_space=pl.ANY)],
        scratch_shapes=[pltpu.VMEM((OWN * BOX, CZ), f32), pltpu.SemaphoreType.DMA],
        compiler_params=vmem(20),
        cost_estimate=cost(1 << 30, 5 << 20),
        name="inner_rows",
    )(x, pot)
    bh, bl, inner_total = pl.pallas_call(
        lambda *refs: inner_band_kernel(planes, *refs),
        out_shape=(
            sds((PB, WIDE, CELLS), bf16),
            sds((PB, WIDE, CELLS), bf16),
            sds((OWN, WIDE), f32),
        ),
        compiler_params=vmem(20),
        cost_estimate=cost(1 << 30, 6 << 20),
        name="inner_band",
    )(low, high, own_start, wide_start, own_bh, own_bl, *inner)
    band, image_out = pl.pallas_call(
        lambda *refs: band_kernel(planes, *refs),
        out_shape=(sds((OWN, CZ), f32), image),
        scratch_shapes=[pltpu.VMEM(v.shape, v.dtype) for v in left],
        compiler_params=vmem(20),
        cost_estimate=cost(1 << 30, 6 << 20),
        name="band",
    )(xs, y_before, y_after, partial, own_start, wide_start, bh, bl, inner_total)

    bands = [band] + [shifted(band, "sub", k) for k in (1, 2, 3)]
    gradient = pl.pallas_call(
        lambda *refs: update_kernel(planes, *refs),
        out_shape=sds((OWN * BOX, CZ), f32),
        scratch_shapes=[
            pltpu.VMEM((PB * OWN, PB * WIDE), bf16),
            pltpu.VMEM((PB * OWN, PB * WIDE), bf16),
            pltpu.VMEM((OWN, WIDE), f32),
        ],
        compiler_params=vmem(20),
        cost_estimate=cost(2 << 30, 5 << 20),
        name="gradient",
    )(
        *bands, image_in, image_out, bh.reshape(PB * WIDE, CELLS), bl.reshape(PB * WIDE, CELLS),
        own_start, wide_start,
    )
    back = exchanged(gradient.reshape(peers, 2, PB, ROWS, CZ))
    return back.reshape(coeffs.shape)


def solution(mesh):
    return jax.shard_map(
        body,
        mesh=mesh,
        in_specs=(P("fn", None, "sub", None), P(), P(None, "sub", None)),
        out_specs=P("fn", None, "sub", None),
        check_vma=False,
    )
```

```python
import jax
import jax.numpy as jnp
from jax import lax
from jax.experimental import pallas as pl
from jax.experimental.pallas import tpu as pltpu
from jax.sharding import PartitionSpec as P

PB = 4
ROWS = 4
CZ = 128
OWN = 128
HALF = 64
HALO = 48
WIDE = 256
CELLS = ROWS * CZ
BOX = PB * ROWS
PENALTY = 0.5
INNER = (1, 2)
OUTER = (0, 3)
ORDER = INNER + OUTER
LINE = 8
VOLUME = 1.0 / (PB * 16 * CZ)


def vmem(mib):
    return pltpu.CompilerParams(vmem_limit_bytes=mib << 20)


def split(x):
    hi = x.astype(jnp.bfloat16)
    lo = (x - hi.astype(jnp.float32)).astype(jnp.bfloat16)
    return hi, lo


def own_rows(ref, first, step):
    return jnp.concatenate(
        [ref[pl.ds(par * step + first, HALF, stride=2 * step), :] for par in range(2)], axis=0
    )


def potential_kernel(starts, potential, out):
    planes = potential.shape[0]

    def one(n, carry):
        first = starts[n]
        for p in range(PB):
            plane = first + p
            plane = jnp.where(plane >= planes, plane - planes, plane)
            v = potential[plane]
            for y in range(ROWS):
                out[pl.ds((p * ROWS + y) * OWN + n, 1), :] = v[y : y + 1, :]
        return carry

    lax.fori_loop(0, OWN, one, 0, unroll=4)


def edge_kernel(x, first, last, low, high):
    at = lax.axis_index("sub")
    for p in range(PB):
        to = slice(p * OWN, (p + 1) * OWN)
        first[to, :] = jnp.where(at == 0, 0.0, own_rows(x, p * ROWS, BOX))
        v = own_rows(x, p * ROWS + ROWS - 1, BOX)
        last[to, :] = jnp.where(at == lax.axis_size("sub") - 1, 0.0, v)
    for k in range(HALO):
        to = slice(k * BOX, (k + 1) * BOX)
        low_at = (HALF - HALO + k) * 2 * BOX + BOX
        low[to, :] = x[low_at : low_at + BOX, :]
        high[to, :] = x[k * 2 * BOX : k * 2 * BOX + BOX, :]


def difference(own_start, wide_start, planes):
    d = wide_start[...] - own_start[...]
    d = jnp.where(d >= planes // 2, d - planes, d)
    return jnp.where(d < -(planes // 2), d + planes, d)


def dot_t(a, b):
    return lax.dot_general(a, b, (((1,), (1,)), ((), ())), preferred_element_type=jnp.float32)


def block(ref, p, y):
    at = (p * ROWS + y) * OWN
    return ref[at : at + OWN, :]


def put(hi_ref, lo_ref, k, cols, v):
    hi, lo = split(v)
    hi_ref[k * OWN : (k + 1) * OWN, cols] = hi
    lo_ref[k * OWN : (k + 1) * OWN, cols] = lo


def act(xs, pot, p, y):
    lane = lax.broadcasted_iota(jnp.int32, (OWN, CZ), 1)
    phi = block(xs, p, y)
    beside = jnp.where(lane == 0, 0.0, pltpu.roll(phi, 1, 1))
    beside = beside + jnp.where(lane == CZ - 1, 0.0, pltpu.roll(phi, CZ - 1, 1))
    if y > 0:
        beside = beside + block(xs, p, y - 1)
    if y < ROWS - 1:
        beside = beside + block(xs, p, y + 1)
    return (3.0 - PENALTY + block(pot, p, y)) * phi - 0.5 * beside


def left_sides(at, phi, acted, image, fh, fl, gh, gl, hh, hl):
    cols = slice(at * CZ, (at + 1) * CZ)
    half = [-0.5 * v for v in phi]
    put(fh, fl, 0, cols, half[0])
    put(fh, fl, 5, cols, half[PB - 1])
    for p in range(PB):
        v = acted[p]
        if p > 0:
            v = v + half[p - 1]
        if p < PB - 1:
            v = v + half[p + 1]
        image[(p * 2 + at) * OWN : (p * 2 + at + 1) * OWN, :] = v
        put(fh, fl, p + 1, cols, v)
    for k in range(3):
        p = k + 1
        put(gh, gl, k, cols, acted[p] if p == PB - 1 else acted[p] + half[p + 1])
        put(hh, hl, k, cols, acted[k] if k == 0 else acted[k] + half[k - 1])


def inner_kernel(x, pot_any, bh, bl, xs, image, partial, fh, fl, gh, gl, hh, hl, pot, sem):
    copy = pltpu.make_async_copy(pot_any, pot, sem)
    copy.start()
    for p in range(PB):
        for at, y in enumerate(ORDER):
            cols = slice(at * CZ, (at + 1) * CZ)
            v = own_rows(x, p * ROWS + y, BOX)
            to = (p * ROWS + y) * OWN
            xs[to : to + OWN, :] = v
            hi, lo = split(v)
            bh[p, :, cols] = hi
            bl[p, :, cols] = lo
    copy.wait()
    for at, y in enumerate(INNER):
        phi = [block(xs, p, y) for p in range(PB)]
        acted = [act(xs, pot, p, y) for p in range(PB)]
        left_sides(at, phi, acted, image, fh, fl, gh, gl, hh, hl)
    for at, y in enumerate(OUTER):
        for p in range(PB):
            partial[(p * 2 + at) * OWN : (p * 2 + at + 1) * OWN, :] = act(xs, pot, p, y)


def outer_rows(xs, y_before, y_after, partial, image, fh, fl, gh, gl, hh, hl):
    for at, (y, beyond) in enumerate(zip(OUTER, (y_before, y_after))):
        phi = [block(xs, p, y) for p in range(PB)]
        acted = [
            partial[(p * 2 + at) * OWN : (p * 2 + at + 1) * OWN, :]
            - 0.5 * beyond[p * OWN : (p + 1) * OWN, :]
            for p in range(PB)
        ]
        left_sides(at, phi, acted, image, fh, fl, gh, gl, hh, hl)


def products(total, apart, bh, bl, side, fh, fl, gh, gl, hh, hl):
    cols = slice(side * 2 * CZ, (side + 1) * 2 * CZ)
    pieces = {
        0: ((fh, fl, 0, 2, -1), (gh, gl, 0, 3, 1)),
        1: ((fh, fl, 0, 6, -1),),
        2: ((fh, fl, 0, 6, -1),),
        3: ((hh, hl, 0, 3, 0), (fh, fl, 4, 2, 3)),
    }
    for q in range(PB):
        right_hi, right_lo = bh[q, :, cols], bl[q, :, cols]
        for hi, lo, at, count, first in pieces[q]:
            rows = slice(at * OWN, (at + count) * OWN)
            r = dot_t(hi[rows, :], right_hi) + dot_t(hi[rows, :], right_lo)
            r = r + dot_t(lo[rows, :], right_hi)
            for k in range(count):
                total = total + jnp.where(
                    apart == first + k - q, r[k * OWN : (k + 1) * OWN, :], 0.0
                )
    return total


def inner_band_kernel(
    planes, low, high, own_start, wide_start, own_bh, own_bl, fh, fl, gh, gl, hh, hl,
    bh, bl, total,
):
    zero = jnp.zeros((16, CELLS), jnp.bfloat16)
    for q in range(PB):
        for ref, own in ((bh, own_bh), (bl, own_bl)):
            ref[q, 0:16, :] = zero
            ref[q, HALF : HALF + OWN, :] = own[q]
            ref[q, WIDE - 16 :, :] = zero
        for at, y in enumerate(ORDER):
            cols = slice(at * CZ, (at + 1) * CZ)
            for ref, to in ((low, 16), (high, HALF + OWN)):
                hi, lo = split(ref[pl.ds(q * ROWS + y, HALO, stride=BOX), :])
                bh[q, to : to + HALO, cols] = hi
                bl[q, to : to + HALO, cols] = lo
    apart = difference(own_start, wide_start, planes)
    start = jnp.zeros((OWN, WIDE), jnp.float32)
    total[...] = products(start, apart, bh, bl, 0, fh, fl, gh, gl, hh, hl)


def band_kernel(
    planes, xs, y_before, y_after, partial, own_start, wide_start, bh, bl, earlier,
    band, image, fh, fl, gh, gl, hh, hl,
):
    outer_rows(xs, y_before, y_after, partial, image, fh, fl, gh, gl, hh, hl)
    apart = difference(own_start, wide_start, planes)
    total = products(earlier[...], apart, bh, bl, 1, fh, fl, gh, gl, hh, hl) * VOLUME
    for b in range(4):
        band[32 * b : 32 * b + 32, :] = total[32 * b : 32 * b + 32, 32 * b + 16 : 32 * b + 144]


def update_kernel(
    planes, b0, b1, b2, b3, image_in, image_out, bh, bl, own_start, wide_start, out, w, wide
):
    band = b0[...] + b1[...] + b2[...] + b3[...]
    for b in range(4):
        parts = [band[32 * b : 32 * b + 32, :]]
        before, after = 32 * b + 16, 112 - 32 * b
        parts = [jnp.zeros((32, before), jnp.float32), *parts, jnp.zeros((32, after), jnp.float32)]
        wide[32 * b : 32 * b + 32, :] = jnp.concatenate(parts, axis=1)
    mixing = wide[...]
    apart = difference(own_start, wide_start, planes)
    for d in range(1 - PB, PB):
        hi, lo = split(jnp.where(apart == d, mixing, 0.0))
        for p in range(PB):
            q = p - d
            if 0 <= q < PB:
                cols = slice(q * WIDE, (q + 1) * WIDE)
                w[p * OWN : (p + 1) * OWN, cols] = hi
                w[(PB + p) * OWN : (PB + p + 1) * OWN, cols] = lo
    def dot(a, b):
        return jnp.dot(a, b, preferred_element_type=jnp.float32)

    both = dot(w[...], bh[...])
    r = both[: PB * OWN, :] + both[PB * OWN :, :] + dot(w[: PB * OWN, :], bl[...])
    for p in range(PB):
        for at, y in enumerate(ORDER):
            image = (image_in, image_out)[at // 2]
            first = (p * 2 + at % 2) * OWN
            v = image[first : first + OWN, :]
            v = v - r[p * OWN : (p + 1) * OWN, at * CZ : (at + 1) * CZ]
            for par in range(2):
                out[pl.ds(par * BOX + p * ROWS + y, HALF, stride=2 * BOX), :] = v[
                    par * HALF : (par + 1) * HALF
                ]


def snake(k):
    return k if k // LINE % 2 == 0 else k // LINE * LINE + LINE - 1 - k % LINE


def shifted(x, axis, step):
    n = lax.axis_size(axis)
    at = snake if axis == "fn" else int
    return lax.ppermute(x, axis, [(at(i), at((i + step) % n)) for i in range(n)])


def exchanged(x):
    order = [snake(k) for k in range(lax.axis_size("fn"))]
    return lax.all_to_all(
        x, "fn", split_axis=0, concat_axis=0, axis_index_groups=[order], tiled=True
    )


def body(coeffs, offsets, potential):
    peers = lax.axis_size("fn")
    position = lax.axis_index("fn")
    planes = potential.shape[0]
    padded = jnp.concatenate([offsets[-HALF:], offsets, offsets[:HALF]])
    line, along = position // LINE, position % LINE
    number = jnp.where(line % 2 == 0, position, line * LINE + LINE - 1 - along)
    wide_start = lax.dynamic_slice(padded, (number * OWN,), (WIDE,)).reshape(-1, 2, LINE)
    wide_start = jnp.stack([wide_start[:, 0], wide_start[:, 1, ::-1]], axis=1).reshape(WIDE)
    own_start = wide_start[HALF : HALF + OWN]
    f32, bf16 = jnp.float32, jnp.bfloat16
    sds = jax.ShapeDtypeStruct

    def cost(flops, size):
        return pl.CostEstimate(flops=flops, bytes_accessed=size, transcendentals=0)

    pot = pl.pallas_call(
        potential_kernel,
        out_shape=sds((OWN * BOX, CZ), f32),
        in_specs=[
            pl.BlockSpec(memory_space=pltpu.SMEM),
            pl.BlockSpec(memory_space=pltpu.VMEM),
        ],
        compiler_params=vmem(10),
        cost_estimate=cost(0, 4 << 20),
        name="box_potential",
    )(own_start, potential)
    wide_start = wide_start[None, :]
    own_start = own_start[:, None]

    x = exchanged(coeffs.reshape(peers, 2 * BOX, CZ))
    x, pot, own_start, wide_start = lax.optimization_barrier((x, pot, own_start, wide_start))
    x = x.reshape(OWN * BOX, CZ)
    edge, halo = sds((OWN * PB, CZ), f32), sds((HALO * BOX, CZ), f32)
    first, last, low, high = pl.pallas_call(
        edge_kernel,
        out_shape=(edge, edge, halo, halo),
        compiler_params=vmem(10),
        cost_estimate=cost(0, 2 << 20),
        name="edges",
    )(x)
    y_before = shifted(last, "sub", 1)
    y_after = shifted(first, "sub", -1)
    low = shifted(low, "fn", 1)
    high = shifted(high, "fn", -1)

    image = sds((PB * 2 * OWN, CZ), f32)
    left = [sds((n * OWN, 2 * CZ), bf16) for n in (6, 6, 3, 3, 3, 3)]
    own = sds((PB, OWN, CELLS), bf16)
    own_bh, own_bl, xs, image_in, partial, *inner = pl.pallas_call(
        inner_kernel,
        out_shape=(own, own, sds((OWN * BOX, CZ), f32), image, image, *left),
        in_specs=[pl.BlockSpec(memory_space=pltpu.VMEM), pl.BlockSpec(memory_space=pl.ANY)],
        scratch_shapes=[pltpu.VMEM((OWN * BOX, CZ), f32), pltpu.SemaphoreType.DMA],
        compiler_params=vmem(20),
        cost_estimate=cost(1 << 30, 5 << 20),
        name="inner_rows",
    )(x, pot)
    bh, bl, inner_total = pl.pallas_call(
        lambda *refs: inner_band_kernel(planes, *refs),
        out_shape=(
            sds((PB, WIDE, CELLS), bf16),
            sds((PB, WIDE, CELLS), bf16),
            sds((OWN, WIDE), f32),
        ),
        compiler_params=vmem(20),
        cost_estimate=cost(1 << 30, 6 << 20),
        name="inner_band",
    )(low, high, own_start, wide_start, own_bh, own_bl, *inner)
    band, image_out = pl.pallas_call(
        lambda *refs: band_kernel(planes, *refs),
        out_shape=(sds((OWN, CZ), f32), image),
        scratch_shapes=[pltpu.VMEM(v.shape, v.dtype) for v in left],
        compiler_params=vmem(20),
        cost_estimate=cost(1 << 30, 6 << 20),
        name="band",
    )(xs, y_before, y_after, partial, own_start, wide_start, bh, bl, inner_total)

    bands = [band] + [shifted(band, "sub", k) for k in (3, 2, 1)]
    gradient = pl.pallas_call(
        lambda *refs: update_kernel(planes, *refs),
        out_shape=sds((OWN * BOX, CZ), f32),
        scratch_shapes=[
            pltpu.VMEM((2 * PB * OWN, PB * WIDE), bf16),
            pltpu.VMEM((OWN, WIDE), f32),
        ],
        compiler_params=vmem(20),
        cost_estimate=cost(2 << 30, 5 << 20),
        name="gradient",
    )(
        *bands, image_in, image_out, bh.reshape(PB * WIDE, CELLS), bl.reshape(PB * WIDE, CELLS),
        own_start, wide_start,
    )
    back = exchanged(gradient.reshape(peers, 2, PB, ROWS, CZ))
    return back.reshape(coeffs.shape)


def solution(mesh):
    return jax.shard_map(
        body,
        mesh=mesh,
        in_specs=(P("fn", None, "sub", None), P(), P(None, "sub", None)),
        out_specs=P("fn", None, "sub", None),
        check_vma=False,
    )
```

```python
import jax
import jax.numpy as jnp
from jax import lax
from jax.experimental import pallas as pl
from jax.experimental.pallas import tpu as pltpu
from jax.sharding import PartitionSpec as P

PB = 4
ROWS = 4
CZ = 128
OWN = 128
HALF = 64
HALO = 48
WIDE = 256
CELLS = ROWS * CZ
BOX = PB * ROWS
PENALTY = 0.5
INNER = (1, 2)
OUTER = (0, 3)
ORDER = INNER + OUTER
LINE = 8
VOLUME = 1.0 / (PB * 16 * CZ)


def vmem(mib):
    return pltpu.CompilerParams(vmem_limit_bytes=mib << 20)


def split(x):
    hi = x.astype(jnp.bfloat16)
    lo = (x - hi.astype(jnp.float32)).astype(jnp.bfloat16)
    return hi, lo


def own_rows(ref, first, step):
    return jnp.concatenate(
        [ref[pl.ds(par * step + first, HALF, stride=2 * step), :] for par in range(2)], axis=0
    )


def potential_kernel(starts, potential, out):
    planes = potential.shape[0]

    def one(n, carry):
        first = starts[n]
        for p in range(PB):
            plane = first + p
            plane = jnp.where(plane >= planes, plane - planes, plane)
            v = potential[plane]
            for y in range(ROWS):
                out[pl.ds((p * ROWS + y) * OWN + n, 1), :] = v[y : y + 1, :]
        return carry

    lax.fori_loop(0, OWN, one, 0, unroll=4)


def edge_kernel(x, first, last, low, high):
    at = lax.axis_index("sub")
    for p in range(PB):
        to = slice(p * OWN, (p + 1) * OWN)
        first[to, :] = jnp.where(at == 0, 0.0, own_rows(x, p * ROWS, BOX))
        v = own_rows(x, p * ROWS + ROWS - 1, BOX)
        last[to, :] = jnp.where(at == lax.axis_size("sub") - 1, 0.0, v)
    for k in range(HALO):
        to = slice(k * BOX, (k + 1) * BOX)
        low_at = (HALF - HALO + k) * 2 * BOX + BOX
        low[to, :] = x[low_at : low_at + BOX, :]
        high[to, :] = x[k * 2 * BOX : k * 2 * BOX + BOX, :]


def difference(own_start, wide_start, planes):
    d = wide_start[...] - own_start[...]
    d = jnp.where(d >= planes // 2, d - planes, d)
    return jnp.where(d < -(planes // 2), d + planes, d)


def dot_t(a, b):
    return lax.dot_general(a, b, (((1,), (1,)), ((), ())), preferred_element_type=jnp.float32)


def block(ref, p, y):
    at = (p * ROWS + y) * OWN
    return ref[at : at + OWN, :]


def put(hi_ref, lo_ref, k, cols, v):
    hi, lo = split(v)
    hi_ref[k * OWN : (k + 1) * OWN, cols] = hi
    lo_ref[k * OWN : (k + 1) * OWN, cols] = lo


def act(xs, pot, p, y):
    lane = lax.broadcasted_iota(jnp.int32, (OWN, CZ), 1)
    phi = block(xs, p, y)
    beside = jnp.where(lane == 0, 0.0, pltpu.roll(phi, 1, 1))
    beside = beside + jnp.where(lane == CZ - 1, 0.0, pltpu.roll(phi, CZ - 1, 1))
    if y > 0:
        beside = beside + block(xs, p, y - 1)
    if y < ROWS - 1:
        beside = beside + block(xs, p, y + 1)
    return (3.0 - PENALTY + block(pot, p, y)) * phi - 0.5 * beside


def left_sides(at, phi, acted, image, fh, fl, gh, gl, hh, hl):
    cols = slice(at * CZ, (at + 1) * CZ)
    half = [-0.5 * v for v in phi]
    put(fh, fl, 0, cols, half[0])
    put(fh, fl, 5, cols, half[PB - 1])
    for p in range(PB):
        v = acted[p]
        if p > 0:
            v = v + half[p - 1]
        if p < PB - 1:
            v = v + half[p + 1]
        image[(p * 2 + at) * OWN : (p * 2 + at + 1) * OWN, :] = v
        put(fh, fl, p + 1, cols, v)
    for k in range(3):
        p = k + 1
        put(gh, gl, k, cols, acted[p] if p == PB - 1 else acted[p] + half[p + 1])
        put(hh, hl, k, cols, acted[k] if k == 0 else acted[k] + half[k - 1])


def inner_kernel(x, pot_any, bh, bl, xs, image, partial, fh, fl, gh, gl, hh, hl, pot, sem):
    copy = pltpu.make_async_copy(pot_any, pot, sem)
    copy.start()
    for p in range(PB):
        for at, y in enumerate(ORDER):
            cols = slice(at * CZ, (at + 1) * CZ)
            v = own_rows(x, p * ROWS + y, BOX)
            to = (p * ROWS + y) * OWN
            xs[to : to + OWN, :] = v
            hi, lo = split(v)
            bh[p, :, cols] = hi
            bl[p, :, cols] = lo
    copy.wait()
    for at, y in enumerate(INNER):
        phi = [block(xs, p, y) for p in range(PB)]
        acted = [act(xs, pot, p, y) for p in range(PB)]
        left_sides(at, phi, acted, image, fh, fl, gh, gl, hh, hl)
    for at, y in enumerate(OUTER):
        for p in range(PB):
            partial[(p * 2 + at) * OWN : (p * 2 + at + 1) * OWN, :] = act(xs, pot, p, y)


def outer_rows(xs, y_before, y_after, partial, image, fh, fl, gh, gl, hh, hl):
    for at, (y, beyond) in enumerate(zip(OUTER, (y_before, y_after))):
        phi = [block(xs, p, y) for p in range(PB)]
        acted = [
            partial[(p * 2 + at) * OWN : (p * 2 + at + 1) * OWN, :]
            - 0.5 * beyond[p * OWN : (p + 1) * OWN, :]
            for p in range(PB)
        ]
        left_sides(at, phi, acted, image, fh, fl, gh, gl, hh, hl)


def products(total, apart, bh, bl, side, fh, fl, gh, gl, hh, hl):
    cols = slice(side * 2 * CZ, (side + 1) * 2 * CZ)
    pieces = {
        0: ((fh, fl, 0, 2, -1), (gh, gl, 0, 3, 1)),
        1: ((fh, fl, 0, 6, -1),),
        2: ((fh, fl, 0, 6, -1),),
        3: ((hh, hl, 0, 3, 0), (fh, fl, 4, 2, 3)),
    }
    for q in range(PB):
        right_hi, right_lo = bh[q, :, cols], bl[q, :, cols]
        for hi, lo, at, count, first in pieces[q]:
            rows = slice(at * OWN, (at + count) * OWN)
            both = dot_t(jnp.concatenate([hi[rows, :], lo[rows, :]], axis=0), right_hi)
            r = both[: count * OWN, :] + both[count * OWN :, :] + dot_t(hi[rows, :], right_lo)
            for k in range(count):
                total = total + jnp.where(
                    apart == first + k - q, r[k * OWN : (k + 1) * OWN, :], 0.0
                )
    return total


def inner_band_kernel(
    planes, low, high, own_start, wide_start, own_bh, own_bl, fh, fl, gh, gl, hh, hl,
    bh, bl, total,
):
    zero = jnp.zeros((16, CELLS), jnp.bfloat16)
    for q in range(PB):
        for ref, own in ((bh, own_bh), (bl, own_bl)):
            ref[q, 0:16, :] = zero
            ref[q, HALF : HALF + OWN, :] = own[q]
            ref[q, WIDE - 16 :, :] = zero
        for at, y in enumerate(ORDER):
            cols = slice(at * CZ, (at + 1) * CZ)
            for ref, to in ((low, 16), (high, HALF + OWN)):
                hi, lo = split(ref[pl.ds(q * ROWS + y, HALO, stride=BOX), :])
                bh[q, to : to + HALO, cols] = hi
                bl[q, to : to + HALO, cols] = lo
    apart = difference(own_start, wide_start, planes)
    start = jnp.zeros((OWN, WIDE), jnp.float32)
    total[...] = products(start, apart, bh, bl, 0, fh, fl, gh, gl, hh, hl)


def band_kernel(
    planes, xs, y_before, y_after, partial, own_start, wide_start, bh, bl, earlier,
    band, image, fh, fl, gh, gl, hh, hl,
):
    outer_rows(xs, y_before, y_after, partial, image, fh, fl, gh, gl, hh, hl)
    apart = difference(own_start, wide_start, planes)
    total = products(earlier[...], apart, bh, bl, 1, fh, fl, gh, gl, hh, hl) * VOLUME
    for b in range(4):
        band[32 * b : 32 * b + 32, :] = total[32 * b : 32 * b + 32, 32 * b + 16 : 32 * b + 144]


def update_kernel(
    planes, b0, b1, b2, b3, image_in, image_out, bh, bl, own_start, wide_start, out, w, wide
):
    band = b0[...] + b1[...] + b2[...] + b3[...]
    for b in range(4):
        parts = [band[32 * b : 32 * b + 32, :]]
        before, after = 32 * b + 16, 112 - 32 * b
        parts = [jnp.zeros((32, before), jnp.float32), *parts, jnp.zeros((32, after), jnp.float32)]
        wide[32 * b : 32 * b + 32, :] = jnp.concatenate(parts, axis=1)
    mixing = wide[...]
    apart = difference(own_start, wide_start, planes)
    for d in range(1 - PB, PB):
        hi, lo = split(jnp.where(apart == d, mixing, 0.0))
        for p in range(PB):
            q = p - d
            if 0 <= q < PB:
                cols = slice(q * WIDE, (q + 1) * WIDE)
                w[p * OWN : (p + 1) * OWN, cols] = hi
                w[(PB + p) * OWN : (PB + p + 1) * OWN, cols] = lo
    def dot(a, b):
        return jnp.dot(a, b, preferred_element_type=jnp.float32)

    both = dot(w[...], bh[...])
    r = both[: PB * OWN, :] + both[PB * OWN :, :] + dot(w[: PB * OWN, :], bl[...])
    for p in range(PB):
        for at, y in enumerate(ORDER):
            image = (image_in, image_out)[at // 2]
            first = (p * 2 + at % 2) * OWN
            v = image[first : first + OWN, :]
            v = v - r[p * OWN : (p + 1) * OWN, at * CZ : (at + 1) * CZ]
            for par in range(2):
                out[pl.ds(par * BOX + p * ROWS + y, HALF, stride=2 * BOX), :] = v[
                    par * HALF : (par + 1) * HALF
                ]


def snake(k):
    return k if k // LINE % 2 == 0 else k // LINE * LINE + LINE - 1 - k % LINE


def shifted(x, axis, step):
    n = lax.axis_size(axis)
    at = snake if axis == "fn" else int
    return lax.ppermute(x, axis, [(at(i), at((i + step) % n)) for i in range(n)])


def exchanged(x):
    order = [snake(k) for k in range(lax.axis_size("fn"))]
    return lax.all_to_all(
        x, "fn", split_axis=0, concat_axis=0, axis_index_groups=[order], tiled=True
    )


def body(coeffs, offsets, potential):
    peers = lax.axis_size("fn")
    position = lax.axis_index("fn")
    planes = potential.shape[0]
    padded = jnp.concatenate([offsets[-HALF:], offsets, offsets[:HALF]])
    line, along = position // LINE, position % LINE
    number = jnp.where(line % 2 == 0, position, line * LINE + LINE - 1 - along)
    wide_start = lax.dynamic_slice(padded, (number * OWN,), (WIDE,)).reshape(-1, 2, LINE)
    wide_start = jnp.stack([wide_start[:, 0], wide_start[:, 1, ::-1]], axis=1).reshape(WIDE)
    own_start = wide_start[HALF : HALF + OWN]
    f32, bf16 = jnp.float32, jnp.bfloat16
    sds = jax.ShapeDtypeStruct

    def cost(flops, size):
        return pl.CostEstimate(flops=flops, bytes_accessed=size, transcendentals=0)

    pot = pl.pallas_call(
        potential_kernel,
        out_shape=sds((OWN * BOX, CZ), f32),
        in_specs=[
            pl.BlockSpec(memory_space=pltpu.SMEM),
            pl.BlockSpec(memory_space=pltpu.VMEM),
        ],
        compiler_params=vmem(10),
        cost_estimate=cost(0, 4 << 20),
        name="box_potential",
    )(own_start, potential)
    wide_start = wide_start[None, :]
    own_start = own_start[:, None]

    x = exchanged(coeffs.reshape(peers, 2 * BOX, CZ))
    x, pot, own_start, wide_start = lax.optimization_barrier((x, pot, own_start, wide_start))
    x = x.reshape(OWN * BOX, CZ)
    edge, halo = sds((OWN * PB, CZ), f32), sds((HALO * BOX, CZ), f32)
    first, last, low, high = pl.pallas_call(
        edge_kernel,
        out_shape=(edge, edge, halo, halo),
        compiler_params=vmem(10),
        cost_estimate=cost(0, 2 << 20),
        name="edges",
    )(x)
    y_before = shifted(last, "sub", 1)
    y_after = shifted(first, "sub", -1)
    low = shifted(low, "fn", 1)
    high = shifted(high, "fn", -1)

    image = sds((PB * 2 * OWN, CZ), f32)
    left = [sds((n * OWN, 2 * CZ), bf16) for n in (6, 6, 3, 3, 3, 3)]
    own = sds((PB, OWN, CELLS), bf16)
    own_bh, own_bl, xs, image_in, partial, *inner = pl.pallas_call(
        inner_kernel,
        out_shape=(own, own, sds((OWN * BOX, CZ), f32), image, image, *left),
        in_specs=[pl.BlockSpec(memory_space=pltpu.VMEM), pl.BlockSpec(memory_space=pl.ANY)],
        scratch_shapes=[pltpu.VMEM((OWN * BOX, CZ), f32), pltpu.SemaphoreType.DMA],
        compiler_params=vmem(20),
        cost_estimate=cost(1 << 30, 5 << 20),
        name="inner_rows",
    )(x, pot)
    bh, bl, inner_total = pl.pallas_call(
        lambda *refs: inner_band_kernel(planes, *refs),
        out_shape=(
            sds((PB, WIDE, CELLS), bf16),
            sds((PB, WIDE, CELLS), bf16),
            sds((OWN, WIDE), f32),
        ),
        compiler_params=vmem(20),
        cost_estimate=cost(1 << 30, 6 << 20),
        name="inner_band",
    )(low, high, own_start, wide_start, own_bh, own_bl, *inner)
    band, image_out = pl.pallas_call(
        lambda *refs: band_kernel(planes, *refs),
        out_shape=(sds((OWN, CZ), f32), image),
        scratch_shapes=[pltpu.VMEM(v.shape, v.dtype) for v in left],
        compiler_params=vmem(20),
        cost_estimate=cost(1 << 30, 6 << 20),
        name="band",
    )(xs, y_before, y_after, partial, own_start, wide_start, bh, bl, inner_total)

    bands = [band] + [shifted(band, "sub", k) for k in (3, 2, 1)]
    gradient = pl.pallas_call(
        lambda *refs: update_kernel(planes, *refs),
        out_shape=sds((OWN * BOX, CZ), f32),
        scratch_shapes=[
            pltpu.VMEM((2 * PB * OWN, PB * WIDE), bf16),
            pltpu.VMEM((OWN, WIDE), f32),
        ],
        compiler_params=vmem(20),
        cost_estimate=cost(2 << 30, 5 << 20),
        name="gradient",
    )(
        *bands, image_in, image_out, bh.reshape(PB * WIDE, CELLS), bl.reshape(PB * WIDE, CELLS),
        own_start, wide_start,
    )
    back = exchanged(gradient.reshape(peers, 2, PB, ROWS, CZ))
    return back.reshape(coeffs.shape)


def solution(mesh):
    return jax.shard_map(
        body,
        mesh=mesh,
        in_specs=(P("fn", None, "sub", None), P(), P(None, "sub", None)),
        out_specs=P("fn", None, "sub", None),
        check_vma=False,
    )
```
